512 devices in a mesh: expert: 128 (over x, z, y_hi, core), replica: 4 (over y_lo).
Axes of the slice: x: 4, y: 8 (y_hi: 2, y_lo: 4; y = y_hi * 4 + y_lo), z: 8, core: 2. Of those that a mesh axis runs over, the one named last changes fastest.
Arguments:
- tokens: bfloat16 [65536, 2048], P(('replica', 'expert')), parts along dimension 0, may hold values from -6 to 6
- expert_ids: int32 [65536, 8], P(('replica', 'expert')), parts along dimension 0, may hold values from 0 to 127, all different within a row; in each aligned block of 128 rows (0 to 127, 128 to 255, ...) at most 12 rows name the same one
- combine: float32 [65536, 8], P(('replica', 'expert')), parts along dimension 0, may hold values from 0.25 to 1
- old_gate: bfloat16 [24576, 2048], P('expert'), may hold values from -0.125 to 0.125
- old_up: bfloat16 [24576, 2048], P('expert'), may hold values from -0.125 to 0.125
- old_down: bfloat16 [24576, 2048], P('expert'), may hold values from -0.21875 to 0.21875
- move_plan: int32 [32, 3, 96], replicated, may hold values from -1 to 191, as said below
Outputs:
- mixed: bfloat16 [65536, 2048], P(('replica', 'expert')), parts along dimension 0
- arrived: bfloat16 [12, 12288, 2048], P('replica', 'expert'), parts along dimension 0
The draws below stay inside these ranges and needn't reach their ends.
There are 4 independent parts, one for each index of `replica`. The reference program is written for one: setup_inputs(seed, part) draws one part's arguments, and reference() takes and returns one part's arrays. A program takes and returns all parts, laid end to end along the dimension named above; an argument that names none is the same for every part. Nothing has to cross between parts.
Inputs may be any that keep to these rules, and one draw needn't show every extreme that they name: `expert_ids`: each row names 8 different experts; among the 128 rows of one device no expert is named more than 12 times, a bound that some block reaches. `move_plan`: in each group the non-negative entries over the three survivors name every one of the leaving device's 192 rows exactly once; each survivor's entries fill its slots from the first, -1 after them; every survivor receives at least 24 rows; in every draw some survivor receives 96 rows.
All inputs are finite; a program needn't handle non-finite values.
Results may differ from the reference program's by a relative error of at most 0.0058.
Values may be sent and summed in bfloat16 or wider, within the bound.
A program may use at most 128 MiB of HBM per device.

```python
import math
import jax
import jax.numpy as jnp
import numpy as np
from jax import lax

D = 2048
HIDDEN_UNITS = 768
EXPERTS_ALL = 128
TOPK = 8
TOK_DEV = 128
TOKENS = 16384
EXPERTS_WIN = 32
OLD_ROWS = 192
MOVE_MAX = 96
CAP = 12
N_EXPERT = 128


def draw_move_plan(key, part):
    key = jax.random.fold_in(key, 7)
    key_perm, key_first, key_second, key_full = jax.random.split(key, 4)
    group_keys = jax.random.split(key_perm, EXPERTS_WIN)
    permutations = jax.vmap(lambda one_key: jax.random.permutation(one_key, OLD_ROWS))(group_keys)
    least_rows = max(1, MOVE_MAX // 4)
    leading_count = jax.random.randint(key_first, (EXPERTS_WIN,), least_rows, MOVE_MAX + 1)
    full_group = jax.random.randint(key_full, (), 0, EXPERTS_WIN)
    leading_count = jnp.where(jnp.arange(EXPERTS_WIN) == full_group, MOVE_MAX, leading_count)
    second_low = jnp.maximum(MOVE_MAX - leading_count, least_rows)
    second_high = jnp.minimum(MOVE_MAX, OLD_ROWS - leading_count - least_rows)
    second_count = jax.random.randint(key_second, (EXPERTS_WIN,), second_low, second_high + 1)
    trailing_count = OLD_ROWS - leading_count - second_count
    counts = jnp.stack([leading_count, second_count, trailing_count], axis=1)
    starts = jnp.stack([jnp.zeros_like(leading_count), leading_count, leading_count + second_count], axis=1)
    slot_range = jnp.arange(MOVE_MAX)
    take_index = jnp.minimum(starts[:, :, None] + slot_range[None, None, :], OLD_ROWS - 1)
    spread = jnp.broadcast_to(permutations[:, None, :], (EXPERTS_WIN, 3, OLD_ROWS))
    chosen = jnp.take_along_axis(spread, take_index, axis=2)
    return jnp.where(slot_range[None, None, :] < counts[:, :, None], chosen, -1).astype(jnp.int32)


def shard_levels(stream_key, extent, pieces, low, largest):
    gain = 1.0
    for dim, blocks in pieces:
        draws = jax.random.uniform(jax.random.fold_in(jax.random.fold_in(stream_key, 6), dim), (blocks,), jnp.float32, low / len(pieces), largest / len(pieces))
        gain = gain * jnp.repeat(jnp.exp(draws), extent[dim] // blocks).reshape((-1,) + (1,) * (len(extent) - 1 - dim))
    return gain


def shared_out(rng, own, number, rows, count, top, most, slope):
    ranking = jax.random.permutation(rng, count)
    crowded, common = shares(count, rows * top, most, slope, True), shares(count, rows * top, most, slope, False)
    places = jnp.arange(count)

    def named(lengths, offset_by):
        used = int((lengths > 0).sum())
        fixed = max(1, used // 4)
        moved = fixed + (places - fixed + offset_by * (used - fixed)) % max(1, count - fixed)
        return jnp.zeros((count,), jnp.int32).at[ranking[jnp.where(places < fixed, places, moved)]].set(jnp.asarray(lengths, jnp.int32))

    lengths = jnp.where(number % 4 == 0, named(crowded, number // 4), named(common, number - number // 4 - 1))
    mixed = jax.random.permutation(jax.random.fold_in(own, 3), count)
    giver, sink = mixed[0:count // 2 * 2:2], mixed[1:count // 2 * 2:2]
    room = jnp.minimum(lengths[giver] - 1, most - lengths[sink]) // 2
    room = jnp.where((giver == ranking[0]) | (sink == ranking[0]) | (lengths[sink] == 0), 0, jnp.maximum(room, 0))
    moved = jax.random.randint(jax.random.fold_in(own, 4), (count // 2,), 0, 1 << 20) % (room + 1)
    lengths = lengths.at[giver].add(-moved).at[sink].add(moved)
    labels = jnp.searchsorted(jnp.cumsum(lengths), jnp.arange(rows * top), side="right").astype(jnp.int32)
    table = labels.reshape(top, rows).T
    table = table[jax.random.permutation(jax.random.fold_in(own, 1), rows)]
    offset_by = jax.random.randint(jax.random.fold_in(own, 2), (rows, 1), 0, top)
    return jnp.take_along_axis(table, (jnp.arange(top)[None, :] + offset_by) % top, axis=1)


def shares(count, total, most, lean, full):
    portions = [(1 << 20) // math.isqrt(standing ** lean) + 1 for standing in range(1, count + 1)]
    largest = most if full else min(most, max(-(-total // count), total * portions[0] // sum(portions)))
    least = 1 if total - largest >= count - 1 else 0
    given, rest = [largest] + [least] * (count - 1), total - largest - least * (count - 1)
    while rest > 0:
        candidates = [i for i in range(1, count) if given[i] < largest] or [i for i in range(1, count) if given[i] < most]
        mass, budget = sum([portions[i] for i in candidates]), rest
        for i in candidates:
            more = min(most - given[i], max(1, budget * portions[i] // mass), rest)
            given[i] = given[i] + more
            rest = rest - more
    return np.array(given)


def gaussian(stream_key, dims, scale, bound, shards=(), held_as=jnp.bfloat16):
    gain = shard_levels(stream_key, dims, shards, -0.22, 0.18) if shards else 1.0
    array = jax.random.normal(stream_key, dims, jnp.float32) * scale * gain
    return jnp.minimum(jnp.maximum(array, -bound), bound).astype(held_as)


def setup_inputs(seed: int = 0, part: int = 0) -> dict:
    splits = jax.random.split(jax.random.key(seed), 8)
    part_splits = jax.random.split(jax.random.fold_in(splits[7], part), 8)
    tokens = gaussian(part_splits[0], (TOKENS, D), 1.0, 6.0, ((0, 128),))
    expert_ids_keys = jax.random.split(jax.random.fold_in(part_splits[1], 1), TOKENS // TOK_DEV)
    expert_ids_turns = jax.random.permutation(jax.random.fold_in(part_splits[1], 3), TOKENS // TOK_DEV)
    expert_ids = jax.vmap(lambda own, number: shared_out(jax.random.fold_in(part_splits[1], 2), own, number, TOK_DEV, EXPERTS_ALL, TOPK, CAP, 2))(expert_ids_keys, expert_ids_turns).reshape((TOKENS, TOPK))
    combine = jnp.clip(0.25 + 0.75 * jax.random.uniform(part_splits[2], (TOKENS, TOPK), jnp.float32) ** shard_levels(part_splits[2], (TOKENS, TOPK), ((0, 128),), -0.2, 0.2), 0.25, 1.0)
    old_gate = gaussian(splits[3], (N_EXPERT * OLD_ROWS, D), D ** -0.5, 0.125, ((0, 128),))
    old_up = gaussian(splits[4], (N_EXPERT * OLD_ROWS, D), D ** -0.5, 0.125, ((0, 128),))
    old_down = gaussian(splits[5], (N_EXPERT * OLD_ROWS, D), HIDDEN_UNITS ** -0.5, 0.21875, ((0, 128),))
    move_plan = draw_move_plan(jax.random.fold_in(splits[7], 71), part)
    return {"tokens": tokens, "expert_ids": expert_ids, "combine": combine, "old_gate": old_gate, "old_up": old_up, "old_down": old_down, "move_plan": move_plan}


def reference(tokens, expert_ids, combine, old_gate, old_up, old_down, move_plan):
    old_all = jnp.stack([old_gate, old_up, old_down], axis=0)
    model_width = tokens.shape[1]
    leaver_base = (jnp.arange(EXPERTS_WIN, dtype=jnp.int32) * 4 + 3) * OLD_ROWS
    plan_rows = (leaver_base[:, None, None] + jnp.maximum(move_plan, 0)).astype(jnp.int32)
    gathered = jnp.take(old_all, plan_rows.reshape(-1), axis=1).reshape(3, EXPERTS_WIN, 3, MOVE_MAX, model_width)
    gathered = jnp.where((move_plan >= 0)[None, :, :, :, None], gathered, jnp.zeros((), old_all.dtype))
    padded = jnp.concatenate([gathered, jnp.zeros((3, EXPERTS_WIN, 1, MOVE_MAX, model_width), old_all.dtype)], axis=2)
    arrived = padded.reshape(3, EXPERTS_WIN * 4 * MOVE_MAX, model_width)

    flat_ids = expert_ids.reshape(-1)
    flat_weights = combine.reshape(-1)
    limit = N_EXPERT * CAP
    numbers = (((1,), (1,)), ((), ()))

    def one_expert(accumulated, expert_number):
        chosen_mask = flat_ids == expert_number
        positions = jnp.nonzero(chosen_mask, size=limit, fill_value=0)[0].astype(jnp.int32)
        live_slot = jnp.arange(limit) < jnp.sum(chosen_mask.astype(jnp.int32))
        token_rows = (positions // TOPK).astype(jnp.int32)
        inputs = jnp.take(tokens, token_rows, axis=0)
        expert_sum = jnp.zeros((limit, model_width), jnp.float32)
        for remaining_device in range(3):
            owning_device = (4 * expert_number + remaining_device).astype(jnp.int32)
            resident = lax.dynamic_slice_in_dim(old_all, (owning_device * OLD_ROWS).astype(jnp.int32), OLD_ROWS, 1)
            extra_rows = lax.dynamic_slice_in_dim(arrived, (owning_device * MOVE_MAX).astype(jnp.int32), MOVE_MAX, 1)
            held_rows = jnp.concatenate([resident, extra_rows], axis=1)
            gate_value = lax.dot_general(inputs, held_rows[0], numbers, preferred_element_type=jnp.float32)
            up_value = lax.dot_general(inputs, held_rows[1], numbers, preferred_element_type=jnp.float32)
            hidden = (jax.nn.silu(gate_value) * up_value).astype(jnp.bfloat16)
            partial_value = jnp.dot(hidden, held_rows[2], preferred_element_type=jnp.float32).astype(jnp.bfloat16)
            partial_value = lax.optimization_barrier(partial_value)
            expert_sum = expert_sum + partial_value.astype(jnp.float32)
        scales = jnp.where(live_slot, jnp.take(flat_weights, positions), jnp.zeros((), flat_weights.dtype))
        contribution = expert_sum * scales[:, None].astype(jnp.float32)
        accumulated = accumulated.at[token_rows].add(contribution)
        return accumulated, None

    start = jnp.zeros((tokens.shape[0], model_width), jnp.float32)
    accumulated, _ = lax.scan(one_expert, start, jnp.arange(EXPERTS_WIN, dtype=jnp.int32))
    return accumulated.astype(jnp.bfloat16), arrived
```

```python
import jax
import jax.numpy as jnp
from jax import lax
from jax.experimental import pallas as pl
from jax.experimental.pallas import tpu as pltpu
from jax.sharding import PartitionSpec as P

MESH = pl.DeviceIdType.MESH
F32 = jnp.float32
BF16 = jnp.bfloat16

X, Z, RING, HALF = 4, 8, 8, 4
EXPERTS = X * Z
TOK = 128
D = 2048
Q = D // 4
WIDE = 3 * Q
CAP = 12
ROWS = 16
OLD = 192
UNITS = 4 * OLD
MOVE = 96
CHUNKS = 6
PIECE = 3 * OLD // 2 // CHUNKS
PER = CHUNKS // 3
BATCH = 16
NT = (((1,), (1,)), ((), ()))


def dot(a, b):
    return jnp.dot(a, b, preferred_element_type=F32)


def dot_nt(a, b):
    return lax.dot_general(a, b, NT, preferred_element_type=F32)


def one_hot(condition):
    return jnp.where(condition, 1.0, 0.0).astype(BF16)


def z_offset(k):
    odd = lax.rem(k, 2)
    return odd * lax.div(k + 1, 2) + (1 - odd) * lax.rem(Z - lax.div(k, 2), Z)


def kernel(
    tok, ids, comb, gate, up, down, plan, mixed, arrived,
    wts, send, recv, outs, ret, hid, x3, lhs, fold, arr,
    own_sem, d_send, d_recv, r_send, r_recv, cross_send, hop_send, hop_recv,
    side_send, side_recv, twin_send, twin_recv, arr_sem,
):
    e = lax.axis_index("expert")
    rep = lax.axis_index("replica")
    low, grp = lax.rem(e, 4), lax.div(e, 4)
    half, core = lax.div(low, 2), lax.rem(low, 2)
    gx, gz = lax.div(grp, Z), lax.rem(grp, Z)
    y = half * HALF + rep
    step = 2 * half - 1
    twin = (e + 1 - 2 * core, rep)

    def peer(o, sign):
        ox, oz = lax.div(o, Z), z_offset(lax.rem(o, Z))
        g = lax.rem(gx + X + sign * ox, X) * Z + lax.rem(gz + Z + sign * oz, Z)
        return (4 * g + low, rep)

    def ring(distance):
        there = lax.rem(y + RING + distance, RING)
        return (4 * grp + 2 * lax.div(there, HALF) + core, lax.rem(there, HALF))

    barrier = pltpu.get_barrier_semaphore()

    def greet(device):
        pl.semaphore_signal(barrier, inc=1, device_id=device, device_id_type=MESH)

    @pl.loop(1, EXPERTS)
    def _(o):
        greet(peer(o, 1))

    greet(twin)
    greet(ring(1))
    greet(ring(-1))

    mats = (gate, up, down)
    own = [
        pltpu.make_async_copy(mats[m], wts.at[m, pl.ds(pl.multiple_of(low * OLD, 16), OLD)], own_sem.at[m])
        for m in range(3)
    ]
    for copy in own:
        copy.start()

    ids_t = jnp.transpose(ids[...])
    row = lax.broadcasted_iota(jnp.int32, (128, 128), 0)
    lane = lax.broadcasted_iota(jnp.int32, (128, 128), 1)
    before = one_hot(row < lane)
    slot = row & 15

    def named(i):
        k = row >> 4
        oz = jnp.where((k & 1) == 1, (k + 1) >> 1, (8 - (k >> 1)) & 7)
        g = ((gx + i) & 3) * Z + ((gz + oz) & 7)
        return [ids_t[k : k + 1, :] == g for k in range(8)]

    def places(hits):
        member = hits[0]
        for hit in hits[1:]:
            member = member | hit
        rank = dot(one_hot(member), before)
        rank = jnp.where(member, rank, -1.0).astype(jnp.int32)
        first = (rank == slot) & (slot < CAP)
        last = [(rank == 3 * (slot - CAP) + b) & (slot >= CAP) for b in range(3)]
        return first, last

    @pl.loop(0, 4)
    def _(i):
        first, last = places(named(i))
        rows = pl.ds(pl.multiple_of(i * 128, 128), 128)
        first = one_hot(first)
        for b in range(3):
            part = dot(first, tok[:, b * Q : (b + 1) * Q]) + dot(one_hot(last[b]), tok[:, WIDE:])
            send[rows, b * Q : (b + 1) * Q] = part.astype(BF16)

    pl.semaphore_wait(barrier, EXPERTS + 2)

    def piece(owner, part, k):
        start = owner * OLD + part * (OLD // 2) + lax.rem(k, PER) * PIECE
        return wts.at[lax.div(k, PER), pl.ds(pl.multiple_of(start, 16), PIECE)]

    def passing(ref, sender, receiver, device):
        return pltpu.make_async_remote_copy(
            src_ref=ref, dst_ref=ref, send_sem=sender, recv_sem=receiver, device_id=device, device_id_type=MESH
        )

    position = (half * rep + (1 - half) * (HALF - 1 - rep), half * (HALF - 1 - rep) + (1 - half) * rep)
    ahead = (ring(step), ring(-step))
    behind = (ring(-step), ring(step))
    far = lax.rem(low + 2, 4)

    def cross(part, k):
        return passing(piece(low, part, k), cross_send.at[part, k], hop_recv.at[part, k], behind[part])

    def hop(part, k):
        return passing(piece(far, part, k), hop_send.at[part, k], hop_recv.at[part, k], ahead[part])

    def side(part, k, owner):
        return passing(piece(owner, part, k), side_send.at[part, k], side_recv.at[part, k], twin)

    def own_side(m, owner):
        ref = wts.at[m, pl.ds(pl.multiple_of(owner * OLD, 16), OLD)]
        return passing(ref, twin_send.at[m], twin_recv.at[m], twin)

    for copy in own:
        copy.wait()

    for part in range(2):
        @pl.when(position[part] == 0)
        def _():
            @pl.loop(0, CHUNKS)
            def _(k):
                cross(part, k).start()

    def parcel(source, target, o, sender, receiver, device):
        rows = pl.ds(pl.multiple_of(o * ROWS, ROWS), ROWS)
        return pltpu.make_async_remote_copy(
            src_ref=source.at[rows], dst_ref=target.at[rows], send_sem=sender.at[o], recv_sem=receiver.at[o],
            device_id=device, device_id_type=MESH,
        )

    def dispatch(o):
        return parcel(send, recv, o, d_send, d_recv, peer(o, 1))

    def give_back(o):
        return parcel(outs, ret, o, r_send, r_recv, peer(o, -1))

    @pl.loop(1, EXPERTS)
    def _(o):
        dispatch(o).start()

    for m in range(3):
        own_side(m, low).start()

    recv[0:ROWS, :] = send[0:ROWS, :]

    comb_t = jnp.transpose(comb[...])

    @pl.loop(0, 4)
    def _(i):
        hits = named(i)
        first, last = places(hits)
        weight = jnp.zeros((128, 128), F32)
        for k in range(8):
            weight = weight + jnp.where(hits[k], comb_t[k : k + 1, :], 0.0)
        columns = pl.ds(pl.multiple_of(i * 128, 128), 128)

        def store(b, at, chosen):
            value = jnp.transpose(jnp.where(chosen, weight, 0.0))
            high = value.astype(BF16)
            lhs[b, at : at + 128, columns] = high
            lhs[b, at + 128 : at + 256, columns] = (value - high.astype(F32)).astype(BF16)

        for b in range(3):
            store(b, 0, first)
            store(b, 256, last[b])

    n_rows = BATCH * ROWS
    low_row = lax.broadcasted_iota(jnp.int32, (n_rows, n_rows), 0)
    high_row = lax.broadcasted_iota(jnp.int32, (n_rows, n_rows), 1)
    same = (low_row >> 4) == (high_row >> 4)
    for b in range(3):
        fold[b] = one_hot(
            same & ((low_row & 15) >= CAP) & ((high_row & 15) == 3 * ((low_row & 15) - CAP) + b)
        )
        fold[3 + b] = one_hot(
            same & ((high_row & 15) >= CAP) & ((low_row & 15) == 3 * ((high_row & 15) - CAP) + b)
        )

    @pl.loop(0, CHUNKS + HALF - 1)
    def _(j):
        for part in range(2):
            k = j - position[part]

            @pl.when((k >= 0) & (k < CHUNKS))
            def _():
                hop(part, k).wait_recv()

                @pl.when(position[part] < HALF - 1)
                def _():
                    hop(part, k).start()

                side(part, k, far).start()

    for m in range(3):
        own_side(m, lax.rem(low + 1, 2) + 2 * half).wait_recv()

    @pl.loop(0, CHUNKS)
    def _(k):
        for part in range(2):
            side(part, k, lax.rem(far + 1, 2) + 2 * (1 - half)).wait_recv()

    out_slot = lax.broadcasted_iota(jnp.int32, (n_rows, Q), 0) & 15

    @pl.loop(0, EXPERTS // BATCH)
    def _(i):
        @pl.loop(0, BATCH)
        def _(j):
            o = i * BATCH + j

            @pl.when(o > 0)
            def _():
                dispatch(o).wait_recv()

        rows = pl.ds(pl.multiple_of(i * n_rows, n_rows), n_rows)
        tail = dot(fold[3], recv[rows, 0:Q])
        for b in range(1, 3):
            tail = tail + dot(fold[3 + b], recv[rows, b * Q : (b + 1) * Q])
        x3[...] = tail.astype(BF16)

        @pl.loop(0, UNITS // 256)
        def _(n):
            units = pl.ds(pl.multiple_of(n * 256, 256), 256)

            def project(m):
                return dot_nt(recv[rows, :], wts[m, units, 0:WIDE]) + dot_nt(x3[...], wts[m, units, WIDE:])

            gate_value = project(0)
            hidden = gate_value / (1.0 + jnp.exp(-gate_value)) * project(1)
            hid[:, units] = hidden.astype(BF16)

        last = dot(hid[...], wts[2, :, WIDE:]).astype(BF16)
        for b in range(3):
            columns = slice(b * Q, (b + 1) * Q)
            value = dot(hid[...], wts[2, :, columns])
            outs[rows, columns] = jnp.where(out_slot < CAP, value, dot(fold[b], last)).astype(BF16)

        @pl.loop(0, BATCH)
        def _(j):
            o = i * BATCH + j

            @pl.when(o > 0)
            def _():
                give_back(o).start()

    ret[0:ROWS, :] = outs[0:ROWS, :]

    mine = plan[grp, pl.ds(lax.rem(low, 3), 1), :]
    wanted = lax.broadcasted_iota(jnp.int32, (OLD, MOVE), 0) == mine
    chosen = jnp.transpose(jnp.where(wanted, jnp.where(low < 3, 1.0, 0.0), 0.0)).astype(BF16)
    for m in range(3):
        for b in range(4):
            columns = slice(b * Q, (b + 1) * Q)
            arr[m, :, columns] = dot(chosen, wts[m, 3 * OLD : 4 * OLD, columns]).astype(BF16)
    arr_copy = pltpu.make_async_copy(arr, arrived, arr_sem)
    arr_copy.start()

    @pl.loop(1, EXPERTS)
    def _(o):
        give_back(o).wait_recv()

    end = jnp.zeros((TOK, Q), F32)
    for b in range(3):
        columns = slice(b * Q, (b + 1) * Q)
        sums = dot(lhs[b], ret[:, columns])
        mixed[:, columns] = (sums[0:128] + sums[128:256]).astype(BF16)
        end = end + (sums[256:384] + sums[384:512])
    mixed[:, WIDE:] = end.astype(BF16)

    @pl.loop(1, EXPERTS)
    def _(o):
        dispatch(o).wait_send()
        give_back(o).wait_send()

    for m in range(3):
        own_side(m, low).wait_send()
    for part in range(2):
        @pl.loop(0, CHUNKS)
        def _(k):
            side(part, k, far).wait_send()

        @pl.when(position[part] == 0)
        def _():
            @pl.loop(0, CHUNKS)
            def _(k):
                cross(part, k).wait_send()

        @pl.when(position[part] < HALF - 1)
        def _():
            @pl.loop(0, CHUNKS)
            def _(k):
                hop(part, k).wait_send()

    arr_copy.wait()


def on_device(tokens, expert_ids, combine, old_gate, old_up, old_down, move_plan):
    vmem = pl.BlockSpec(memory_space=pltpu.VMEM)
    hbm = pl.BlockSpec(memory_space=pl.ANY)
    dma = pltpu.SemaphoreType.DMA
    total = EXPERTS * ROWS
    return pl.pallas_call(
        kernel,
        out_shape=(
            jax.ShapeDtypeStruct((TOK, D), BF16),
            jax.ShapeDtypeStruct((3, MOVE, D), BF16),
        ),
        in_specs=[vmem, vmem, vmem, hbm, hbm, hbm, vmem],
        out_specs=(vmem, hbm),
        scratch_shapes=[
            pltpu.VMEM((3, UNITS, D), BF16),
            pltpu.VMEM((total, WIDE), BF16),
            pltpu.VMEM((total, WIDE), BF16),
            pltpu.VMEM((total, WIDE), BF16),
            pltpu.VMEM((total, WIDE), BF16),
            pltpu.VMEM((BATCH * ROWS, UNITS), BF16),
            pltpu.VMEM((BATCH * ROWS, Q), BF16),
            pltpu.VMEM((3, 512, total), BF16),
            pltpu.VMEM((6, BATCH * ROWS, BATCH * ROWS), BF16),
            pltpu.VMEM((3, MOVE, D), BF16),
            dma((3,)),
            dma((EXPERTS,)),
            dma((EXPERTS,)),
            dma((EXPERTS,)),
            dma((EXPERTS,)),
            dma((2, CHUNKS)),
            dma((2, CHUNKS)),
            dma((2, CHUNKS)),
            dma((2, CHUNKS)),
            dma((2, CHUNKS)),
            dma((3,)),
            dma((3,)),
            dma,
        ],
        compiler_params=pltpu.CompilerParams(
            collective_id=0, has_side_effects=True, vmem_limit_bytes=48 * 1024 * 1024
        ),
        name="moe",
    )(tokens, expert_ids, combine, old_gate, old_up, old_down, move_plan)


def solution(mesh):
    placed = (
        P(("replica", "expert"), None),
        P(("replica", "expert"), None),
        P(("replica", "expert"), None),
        P("expert", None),
        P("expert", None),
        P("expert", None),
        P(),
    )
    return jax.shard_map(
        on_device,
        mesh=mesh,
        in_specs=placed,
        out_specs=(P(("replica", "expert"), None), P("replica", "expert", None)),
        check_vma=False,
    )
```

```python
import jax
import jax.numpy as jnp
from jax import lax
from jax.experimental import pallas as pl
from jax.experimental.pallas import tpu as pltpu
from jax.sharding import PartitionSpec as P

MESH = pl.DeviceIdType.MESH
F32 = jnp.float32
BF16 = jnp.bfloat16

X, Z, RING, HALF = 4, 8, 8, 4
EXPERTS = X * Z
TOK = 128
D = 2048
Q = D // 4
WIDE = 3 * Q
CAP = 12
ROWS = 16
OLD = 192
UNITS = 4 * OLD
MOVE = 96
CHUNKS = 18
PIECE = 3 * OLD // 2 // CHUNKS
PER = CHUNKS // 3
SKEW = 3
BATCH = 8
NT = (((1,), (1,)), ((), ()))


def dot(a, b):
    return jnp.dot(a, b, preferred_element_type=F32)


def dot_nt(a, b):
    return lax.dot_general(a, b, NT, preferred_element_type=F32)


def one_hot(condition):
    return jnp.where(condition, 1.0, 0.0).astype(BF16)


def z_offset(k):
    odd = lax.rem(k, 2)
    return odd * lax.div(k + 1, 2) + (1 - odd) * lax.rem(Z - lax.div(k, 2), Z)


def kernel(
    tokens, expert_ids, combine, gate, up, down, move_plan, mixed, arrived,
    ids, comb, plan, tok, wts, send, recv, outs, ret, hid, x3, lhs, fold, arr, acc,
    in_sem, own_sem, d_send, d_recv, r_send, r_recv, cross_send, hop_send, hop_recv,
    side_send, side_recv, twin_send, twin_recv, arr_sem,
):
    e = lax.axis_index("expert")
    rep = lax.axis_index("replica")
    low, grp = lax.rem(e, 4), lax.div(e, 4)
    half, core = lax.div(low, 2), lax.rem(low, 2)
    gx, gz = lax.div(grp, Z), lax.rem(grp, Z)
    y = half * HALF + rep
    step = 2 * half - 1
    twin = (e + 1 - 2 * core, rep)

    def peer(o, sign):
        ox, oz = lax.div(o, Z), z_offset(lax.rem(o, Z))
        g = lax.rem(gx + X + sign * ox, X) * Z + lax.rem(gz + Z + sign * oz, Z)
        return (4 * g + low, rep)

    def ring(distance):
        there = lax.rem(y + RING + distance, RING)
        return (4 * grp + 2 * lax.div(there, HALF) + core, lax.rem(there, HALF))

    mats = (gate, up, down)
    fetched = [
        pltpu.make_async_copy(source, target, in_sem.at[i])
        for i, (source, target) in enumerate(((expert_ids, ids), (tokens, tok), (combine, comb), (move_plan, plan)))
    ]
    own = [
        pltpu.make_async_copy(mats[m], wts.at[m, pl.ds(pl.multiple_of(low * OLD, 16), OLD)], own_sem.at[m])
        for m in range(3)
    ]
    for copy in fetched + own:
        copy.start()

    barrier = pltpu.get_barrier_semaphore()

    def greet(device):
        pl.semaphore_signal(barrier, inc=1, device_id=device, device_id_type=MESH)

    @pl.loop(1, EXPERTS)
    def _(o):
        greet(peer(o, 1))

    greet(twin)
    greet(ring(1))
    greet(ring(-1))

    fetched[0].wait()
    ids_t = ids[...]
    row = lax.broadcasted_iota(jnp.int32, (128, 128), 0)
    lane = lax.broadcasted_iota(jnp.int32, (128, 128), 1)
    before = one_hot(row < lane)
    slot = row & 15

    def named(i):
        k = row >> 4
        oz = jnp.where((k & 1) == 1, (k + 1) >> 1, (8 - (k >> 1)) & 7)
        g = ((gx + i) & 3) * Z + ((gz + oz) & 7)
        return [ids_t[k : k + 1, :] == g for k in range(8)]

    def places(hits):
        member = hits[0]
        for hit in hits[1:]:
            member = member | hit
        rank = dot(one_hot(member), before)
        rank = jnp.where(member, rank, -1.0).astype(jnp.int32)
        first = (rank == slot) & (slot < CAP)
        last = [(rank == 3 * (slot - CAP) + b) & (slot >= CAP) for b in range(3)]
        return first, last

    fetched[1].wait()

    @pl.loop(0, 4)
    def _(i):
        first, last = places(named(i))
        rows = pl.ds(pl.multiple_of(i * 128, 128), 128)
        first = one_hot(first)
        for b in range(3):
            part = dot(first, tok[:, b * Q : (b + 1) * Q]) + dot(one_hot(last[b]), tok[:, WIDE:])
            send[rows, b * Q : (b + 1) * Q] = part.astype(BF16)

    pl.semaphore_wait(barrier, EXPERTS + 2)

    def piece(owner, part, k):
        start = owner * OLD + part * (OLD // 2) + lax.rem(k, PER) * PIECE
        return wts.at[lax.div(k, PER), pl.ds(pl.multiple_of(start, 16), PIECE)]

    def passing(ref, sender, receiver, device):
        return pltpu.make_async_remote_copy(
            src_ref=ref, dst_ref=ref, send_sem=sender, recv_sem=receiver, device_id=device, device_id_type=MESH
        )

    position = (half * rep + (1 - half) * (HALF - 1 - rep), half * (HALF - 1 - rep) + (1 - half) * rep)
    ahead = (ring(step), ring(-step))
    behind = (ring(-step), ring(step))
    far = lax.rem(low + 2, 4)

    def cross(part, k):
        return passing(piece(low, part, k), cross_send.at[part, k], hop_recv.at[part, k], behind[part])

    def hop(part, k):
        return passing(piece(far, part, k), hop_send.at[part, k], hop_recv.at[part, k], ahead[part])

    def side(part, k, owner):
        return passing(piece(owner, part, k), side_send.at[part, k], side_recv.at[part, k], twin)

    def own_side(m, owner):
        ref = wts.at[m, pl.ds(pl.multiple_of(owner * OLD, 16), OLD)]
        return passing(ref, twin_send.at[m], twin_recv.at[m], twin)

    for copy in own:
        copy.wait()

    for part in range(2):
        @pl.when(position[part] == 0)
        def _():
            @pl.loop(0, CHUNKS)
            def _(k):
                cross(part, k).start()

    def parcel(source, target, o, sender, receiver, device):
        rows = pl.ds(pl.multiple_of(o * ROWS, ROWS), ROWS)
        return pltpu.make_async_remote_copy(
            src_ref=source.at[rows], dst_ref=target.at[rows], send_sem=sender.at[o], recv_sem=receiver.at[o],
            device_id=device, device_id_type=MESH,
        )

    def dispatch(o):
        return parcel(send, recv, o, d_send, d_recv, peer(o, 1))

    def give_back(o):
        return parcel(outs, ret, o, r_send, r_recv, peer(o, -1))

    @pl.loop(1, EXPERTS)
    def _(o):
        dispatch(o).start()

    for m in range(3):
        own_side(m, low).start()

    recv[0:ROWS, :] = send[0:ROWS, :]

    fetched[2].wait()
    comb_t = comb[...]

    @pl.loop(0, 4)
    def _(i):
        hits = named(i)
        first, last = places(hits)
        weight = jnp.zeros((128, 128), F32)
        for k in range(8):
            weight = weight + jnp.where(hits[k], comb_t[k : k + 1, :], 0.0)
        columns = pl.ds(pl.multiple_of(i * 128, 128), 128)

        def store(b, at, chosen):
            value = jnp.transpose(jnp.where(chosen, weight, 0.0))
            high = value.astype(BF16)
            lhs[b, at : at + 128, columns] = high
            lhs[b, at + 128 : at + 256, columns] = (value - high.astype(F32)).astype(BF16)

        for b in range(3):
            store(b, 0, first)
            store(b, 256, last[b])

    n_rows = BATCH * ROWS
    low_row = lax.broadcasted_iota(jnp.int32, (n_rows, n_rows), 0)
    high_row = lax.broadcasted_iota(jnp.int32, (n_rows, n_rows), 1)
    same = (low_row >> 4) == (high_row >> 4)
    for b in range(3):
        fold[b] = one_hot(
            same & ((low_row & 15) >= CAP) & ((high_row & 15) == 3 * ((low_row & 15) - CAP) + b)
        )
        fold[3 + b] = one_hot(
            same & ((high_row & 15) >= CAP) & ((low_row & 15) == 3 * ((high_row & 15) - CAP) + b)
        )

    @pl.loop(0, CHUNKS + SKEW * (HALF - 1))
    def _(j):
        for part in range(2):
            k = j - SKEW * position[part]

            @pl.when((k >= 0) & (k < CHUNKS))
            def _():
                hop(part, k).wait_recv()

                @pl.when(position[part] < HALF - 1)
                def _():
                    hop(part, k).start()

                side(part, k, far).start()

    for m in range(3):
        own_side(m, lax.rem(low + 1, 2) + 2 * half).wait_recv()

    @pl.loop(0, CHUNKS)
    def _(k):
        for part in range(2):
            side(part, k, lax.rem(far + 1, 2) + 2 * (1 - half)).wait_recv()

    out_slot = lax.broadcasted_iota(jnp.int32, (n_rows, Q), 0) & 15

    @pl.loop(0, EXPERTS // BATCH)
    def _(i):
        @pl.loop(0, BATCH)
        def _(j):
            o = i * BATCH + j

            @pl.when(o > 0)
            def _():
                dispatch(o).wait_recv()

        rows = pl.ds(pl.multiple_of(i * n_rows, n_rows), n_rows)
        tail = dot(fold[3], recv[rows, 0:Q])
        for b in range(1, 3):
            tail = tail + dot(fold[3 + b], recv[rows, b * Q : (b + 1) * Q])
        x3[...] = tail.astype(BF16)

        @pl.loop(0, UNITS // 256)
        def _(n):
            units = pl.ds(pl.multiple_of(n * 256, 256), 256)

            def project(m):
                return dot_nt(recv[rows, :], wts[m, units, 0:WIDE]) + dot_nt(x3[...], wts[m, units, WIDE:])

            gate_value = project(0)
            hidden = gate_value / (1.0 + jnp.exp(-gate_value)) * project(1)
            hid[:, units] = hidden.astype(BF16)

        last = dot(hid[...], wts[2, :, WIDE:]).astype(BF16)
        for b in range(3):
            columns = slice(b * Q, (b + 1) * Q)
            value = dot(hid[...], wts[2, :, columns])
            outs[rows, columns] = jnp.where(out_slot < CAP, value, dot(fold[b], last)).astype(BF16)

        @pl.loop(0, BATCH)
        def _(j):
            o = i * BATCH + j

            @pl.when(o > 0)
            def _():
                give_back(o).start()

    ret[0:ROWS, :] = outs[0:ROWS, :]

    fetched[3].wait()
    mine = plan[lax.rem(low, 3), pl.ds(grp, 1), :]
    wanted = lax.broadcasted_iota(jnp.int32, (OLD, MOVE), 0) == mine
    chosen = jnp.transpose(jnp.where(wanted, jnp.where(low < 3, 1.0, 0.0), 0.0)).astype(BF16)
    for m in range(3):
        for b in range(4):
            columns = slice(b * Q, (b + 1) * Q)
            arr[m, :, columns] = dot(chosen, wts[m, 3 * OLD : 4 * OLD, columns]).astype(BF16)
    arr_copy = pltpu.make_async_copy(arr, arrived, arr_sem)
    arr_copy.start()

    acc[...] = jnp.zeros_like(acc)

    @pl.loop(0, EXPERTS // BATCH)
    def _(i):
        @pl.loop(0, BATCH)
        def _(j):
            o = i * BATCH + j

            @pl.when(o > 0)
            def _():
                give_back(o).wait_recv()

        rows = pl.ds(pl.multiple_of(i * n_rows, n_rows), n_rows)
        end = acc[:, WIDE:]
        for b in range(3):
            columns = slice(b * Q, (b + 1) * Q)
            sums = dot(lhs[b, :, rows], ret[rows, columns])
            acc[:, columns] = acc[:, columns] + (sums[0:128] + sums[128:256])
            end = end + (sums[256:384] + sums[384:512])
        acc[:, WIDE:] = end

    mixed[...] = acc[...].astype(BF16)

    @pl.loop(1, EXPERTS)
    def _(o):
        dispatch(o).wait_send()
        give_back(o).wait_send()

    for m in range(3):
        own_side(m, low).wait_send()
    for part in range(2):
        @pl.loop(0, CHUNKS)
        def _(k):
            side(part, k, far).wait_send()

        @pl.when(position[part] == 0)
        def _():
            @pl.loop(0, CHUNKS)
            def _(k):
                cross(part, k).wait_send()

        @pl.when(position[part] < HALF - 1)
        def _():
            @pl.loop(0, CHUNKS)
            def _(k):
                hop(part, k).wait_send()

    arr_copy.wait()


def on_device(tokens, expert_ids, combine, old_gate, old_up, old_down, move_plan):
    vmem = pl.BlockSpec(memory_space=pltpu.VMEM)
    hbm = pl.BlockSpec(memory_space=pltpu.HBM)
    dma = pltpu.SemaphoreType.DMA
    total = EXPERTS * ROWS

    def stay(array):
        return pltpu.with_memory_space_constraint(array, pltpu.HBM)

    return pl.pallas_call(
        kernel,
        out_shape=(
            jax.ShapeDtypeStruct((TOK, D), BF16),
            jax.ShapeDtypeStruct((3, MOVE, D), BF16),
        ),
        in_specs=[hbm] * 7,
        out_specs=(vmem, hbm),
        scratch_shapes=[
            pltpu.VMEM((8, TOK), jnp.int32),
            pltpu.VMEM((8, TOK), F32),
            pltpu.VMEM((3, EXPERTS, MOVE), jnp.int32),
            pltpu.VMEM((TOK, D), BF16),
            pltpu.VMEM((3, UNITS, D), BF16),
            pltpu.VMEM((total, WIDE), BF16),
            pltpu.VMEM((total, WIDE), BF16),
            pltpu.VMEM((total, WIDE), BF16),
            pltpu.VMEM((total, WIDE), BF16),
            pltpu.VMEM((BATCH * ROWS, UNITS), BF16),
            pltpu.VMEM((BATCH * ROWS, Q), BF16),
            pltpu.VMEM((3, 512, total), BF16),
            pltpu.VMEM((6, BATCH * ROWS, BATCH * ROWS), BF16),
            pltpu.VMEM((3, MOVE, D), BF16),
            pltpu.VMEM((TOK, D), F32),
            dma((4,)),
            dma((3,)),
            dma((EXPERTS,)),
            dma((EXPERTS,)),
            dma((EXPERTS,)),
            dma((EXPERTS,)),
            dma((2, CHUNKS)),
            dma((2, CHUNKS)),
            dma((2, CHUNKS)),
            dma((2, CHUNKS)),
            dma((2, CHUNKS)),
            dma((3,)),
            dma((3,)),
            dma,
        ],
        compiler_params=pltpu.CompilerParams(
            collective_id=0, has_side_effects=True, vmem_limit_bytes=30 * 1024 * 1024
        ),
        name="moe",
    )(
        stay(tokens), stay(expert_ids.T), stay(combine.T), stay(old_gate), stay(old_up), stay(old_down),
        stay(jnp.transpose(move_plan, (1, 0, 2))),
    )


def solution(mesh):
    placed = (
        P(("replica", "expert"), None),
        P(("replica", "expert"), None),
        P(("replica", "expert"), None),
        P("expert", None),
        P("expert", None),
        P("expert", None),
        P(),
    )
    return jax.shard_map(
        on_device,
        mesh=mesh,
        in_specs=placed,
        out_specs=(P(("replica", "expert"), None), P("replica", "expert", None)),
        check_vma=False,
    )
```

```python
import jax
import jax.numpy as jnp
from jax import lax
from jax.experimental import pallas as pl
from jax.experimental.pallas import tpu as pltpu
from jax.sharding import PartitionSpec as P

MESH = pl.DeviceIdType.MESH
F32 = jnp.float32
BF16 = jnp.bfloat16

X, Z, RING, HALF = 4, 8, 8, 4
EXPERTS = X * Z
TOK = 128
D = 2048
Q = D // 4
WIDE = 3 * Q
CAP = 12
ROWS = 16
OLD = 192
UNITS = 4 * OLD
MOVE = 96
PIECES = 18
PIECE = 16
PER = OLD // 2 // PIECE
TAIL = 3
FULL = PIECES - TAIL
LONG = PIECES + TAIL
EARLY = 2 * PER
SKEW = 3
BATCH = 8
NT = (((1,), (1,)), ((), ()))


def dot(a, b):
    return jnp.dot(a, b, preferred_element_type=F32)


def dot_nt(a, b):
    return lax.dot_general(a, b, NT, preferred_element_type=F32)


def one_hot(condition):
    return jnp.where(condition, 1.0, 0.0).astype(BF16)


def z_offset(k):
    odd = lax.rem(k, 2)
    return odd * lax.div(k + 1, 2) + (1 - odd) * lax.rem(Z - lax.div(k, 2), Z)


def kernel(
    tokens, expert_ids, combine, gate, up, down, move_plan, mixed, arrived,
    ids, comb, plan, tok, wts, send, recv, outs, ret, hid, x3, lhs, fold, arr, acc,
    in_sem, own_sem, d_send, d_recv, r_send, r_recv, cross_send, hop_send, hop_recv,
    side_send, side_recv, twin_send, twin_recv, arr_sem,
):
    e = lax.axis_index("expert")
    rep = lax.axis_index("replica")
    low, grp = lax.rem(e, 4), lax.div(e, 4)
    half, core = lax.div(low, 2), lax.rem(low, 2)
    gx, gz = lax.div(grp, Z), lax.rem(grp, Z)
    y = half * HALF + rep
    step = 2 * half - 1
    twin = (e + 1 - 2 * core, rep)

    def peer(o, sign):
        ox, oz = lax.div(o, Z), z_offset(lax.rem(o, Z))
        g = lax.rem(gx + X + sign * ox, X) * Z + lax.rem(gz + Z + sign * oz, Z)
        return (4 * g + low, rep)

    def ring(distance):
        there = lax.rem(y + RING + distance, RING)
        return (4 * grp + 2 * lax.div(there, HALF) + core, lax.rem(there, HALF))

    mats = (gate, up, down)
    fetched = [
        pltpu.make_async_copy(source, target, in_sem.at[i])
        for i, (source, target) in enumerate(((expert_ids, ids), (tokens, tok), (combine, comb), (move_plan, plan)))
    ]
    own = [
        pltpu.make_async_copy(mats[m], wts.at[m, pl.ds(pl.multiple_of(low * OLD, 16), OLD)], own_sem.at[m])
        for m in range(3)
    ]
    for copy in fetched + own:
        copy.start()

    barrier = pltpu.get_barrier_semaphore()

    def greet(device):
        pl.semaphore_signal(barrier, inc=1, device_id=device, device_id_type=MESH)

    @pl.loop(1, EXPERTS)
    def _(o):
        greet(peer(o, 1))

    greet(twin)
    greet(ring(1))
    greet(ring(-1))

    fetched[0].wait()
    ids_t = ids[...]
    row = lax.broadcasted_iota(jnp.int32, (128, 128), 0)
    lane = lax.broadcasted_iota(jnp.int32, (128, 128), 1)
    before = one_hot(row < lane)
    slot = row & 15

    def named(i):
        k = row >> 4
        oz = jnp.where((k & 1) == 1, (k + 1) >> 1, (8 - (k >> 1)) & 7)
        g = ((gx + i) & 3) * Z + ((gz + oz) & 7)
        return [ids_t[k : k + 1, :] == g for k in range(8)]

    def places(hits):
        member = hits[0]
        for hit in hits[1:]:
            member = member | hit
        rank = dot(one_hot(member), before)
        rank = jnp.where(member, rank, -1.0).astype(jnp.int32)
        first = (rank == slot) & (slot < CAP)
        last = [(rank == 3 * (slot - CAP) + b) & (slot >= CAP) for b in range(3)]
        return first, last

    fetched[1].wait()

    @pl.loop(0, 4)
    def _(i):
        first, last = places(named(i))
        rows = pl.ds(pl.multiple_of(i * 128, 128), 128)
        first = one_hot(first)
        for b in range(3):
            part = dot(first, tok[:, b * Q : (b + 1) * Q]) + dot(one_hot(last[b]), tok[:, WIDE:])
            send[rows, b * Q : (b + 1) * Q] = part.astype(BF16)

    n_rows = BATCH * ROWS
    low_row = lax.broadcasted_iota(jnp.int32, (n_rows, n_rows), 0)
    high_row = lax.broadcasted_iota(jnp.int32, (n_rows, n_rows), 1)
    same = (low_row >> 4) == (high_row >> 4)
    for b in range(3):
        fold[b] = one_hot(
            same & ((low_row & 15) >= CAP) & ((high_row & 15) == 3 * ((low_row & 15) - CAP) + b)
        )
        fold[3 + b] = one_hot(
            same & ((high_row & 15) >= CAP) & ((low_row & 15) == 3 * ((high_row & 15) - CAP) + b)
        )

    pl.semaphore_wait(barrier, EXPERTS + 2)

    def piece(owner, d, q):
        tail = q >= FULL
        extra = lax.max(q - FULL, 0)
        part = jnp.where(tail, lax.rem(extra, 2), d)
        k = jnp.where(tail, FULL + lax.div(extra, 2), q)
        start = owner * OLD + part * (OLD // 2) + lax.rem(k, PER) * PIECE
        return wts.at[lax.div(k, PER), pl.ds(pl.multiple_of(start, PIECE), PIECE)]

    def passing(ref, sender, receiver, device):
        return pltpu.make_async_remote_copy(
            src_ref=ref, dst_ref=ref, send_sem=sender, recv_sem=receiver, device_id=device, device_id_type=MESH
        )

    position = (half * rep + (1 - half) * (HALF - 1 - rep), half * (HALF - 1 - rep) + (1 - half) * rep)
    ahead = (ring(step), ring(-step))
    behind = (ring(-step), ring(step))
    far = lax.rem(low + 2, 4)

    def cross(d, q):
        return passing(piece(low, d, q), cross_send.at[d, q], hop_recv.at[d, q], behind[d])

    def hop(d, q):
        return passing(piece(far, d, q), hop_send.at[d, q], hop_recv.at[d, q], ahead[d])

    def side(d, q, owner):
        return passing(piece(owner, d, q), side_send.at[d, q], side_recv.at[d, q], twin)

    def reaches(d, q):
        return (q >= 0) & (q < LONG) & ((q < FULL) | (position[d] < 2))

    def forwards(d, q):
        return (position[d] == 0) | ((position[d] < HALF - 1) & (q < FULL))

    def own_side(m, owner):
        ref = wts.at[m, pl.ds(pl.multiple_of(owner * OLD, 16), OLD)]
        return passing(ref, twin_send.at[m], twin_recv.at[m], twin)

    for copy in own:
        copy.wait()

    for d in range(2):
        @pl.when(position[d] == 0)
        def _():
            @pl.loop(0, LONG)
            def _(q):
                cross(d, q).start()

    def parcel(source, target, o, sender, receiver, device):
        rows = pl.ds(pl.multiple_of(o * ROWS, ROWS), ROWS)
        return pltpu.make_async_remote_copy(
            src_ref=source.at[rows], dst_ref=target.at[rows], send_sem=sender.at[o], recv_sem=receiver.at[o],
            device_id=device, device_id_type=MESH,
        )

    def dispatch(o):
        return parcel(send, recv, o, d_send, d_recv, peer(o, 1))

    def give_back(o):
        return parcel(outs, ret, o, r_send, r_recv, peer(o, -1))

    @pl.loop(1, BATCH)
    def _(o):
        dispatch(o).start()

    for m in range(3):
        own_side(m, low).start()

    recv[0:ROWS, :] = send[0:ROWS, :]

    @pl.loop(0, FULL + SKEW * (HALF - 1))
    def _(j):
        for d in range(2):
            q = j - SKEW * position[d]

            @pl.when(reaches(d, q))
            def _():
                hop(d, q).wait_recv()

                @pl.when(forwards(d, q))
                def _():
                    hop(d, q).start()

                side(d, q, far).start()

        @pl.when(j < (EXPERTS - BATCH) // 4)
        def _():
            for o in range(4):
                dispatch(BATCH + 4 * j + o).start()

    twin_low, twin_far = lax.rem(low + 1, 2) + 2 * half, lax.rem(far + 1, 2) + 2 * (1 - half)

    def side_waits(first, last):
        @pl.loop(first, last)
        def _(q):
            for d in range(2):
                @pl.when(reaches(d, q))
                def _():
                    side(d, q, twin_far).wait_recv()

    def batch_rows(i):
        return pl.ds(pl.multiple_of(i * n_rows, n_rows), n_rows)

    for m in range(2):
        own_side(m, twin_low).wait_recv()
    side_waits(0, EARLY)

    tiles = UNITS // 256
    out_slot = lax.broadcasted_iota(jnp.int32, (n_rows, Q), 0) & 15

    @pl.loop(0, EXPERTS // BATCH)
    def _(i):
        @pl.loop(0, BATCH)
        def _(j):
            o = i * BATCH + j

            @pl.when(o > 0)
            def _():
                dispatch(o).wait_recv()

        rows = batch_rows(i)
        tail = dot(fold[3], recv[rows, 0:Q])
        for b in range(1, 3):
            tail = tail + dot(fold[3 + b], recv[rows, b * Q : (b + 1) * Q])
        x3[...] = tail.astype(BF16)

        @pl.loop(0, tiles)
        def _(n):
            units = pl.ds(pl.multiple_of(n * 256, 256), 256)

            def project(m):
                return dot_nt(recv[rows, :], wts[m, units, 0:WIDE]) + dot_nt(x3[...], wts[m, units, WIDE:])

            gate_value = project(0)
            hidden = gate_value / (1.0 + jnp.exp(-gate_value)) * project(1)
            hid[:, units] = hidden.astype(BF16)

        @pl.when(i == 0)
        def _():
            own_side(2, twin_low).wait_recv()
            side_waits(EARLY, LONG)

        last = dot(hid[...], wts[2, :, WIDE:]).astype(BF16)
        for b in range(3):
            columns = slice(b * Q, (b + 1) * Q)
            value = dot(hid[...], wts[2, :, columns])
            outs[rows, columns] = jnp.where(out_slot < CAP, value, dot(fold[b], last)).astype(BF16)

        @pl.loop(0, BATCH)
        def _(j):
            o = i * BATCH + j

            @pl.when(o > 0)
            def _():
                give_back(o).start()

    ret[0:ROWS, :] = outs[0:ROWS, :]

    fetched[2].wait()
    comb_t = comb[...]

    @pl.loop(0, 4)
    def _(i):
        hits = named(i)
        first, last = places(hits)
        weight = jnp.zeros((128, 128), F32)
        for k in range(8):
            weight = weight + jnp.where(hits[k], comb_t[k : k + 1, :], 0.0)
        columns = pl.ds(pl.multiple_of(i * 128, 128), 128)

        def store(b, at, chosen):
            value = jnp.transpose(jnp.where(chosen, weight, 0.0))
            high = value.astype(BF16)
            lhs[b, at : at + 128, columns] = high
            lhs[b, at + 128 : at + 256, columns] = (value - high.astype(F32)).astype(BF16)

        for b in range(3):
            store(b, 0, first)
            store(b, 256, last[b])

    fetched[3].wait()
    mine = plan[lax.rem(low, 3), pl.ds(grp, 1), :]
    wanted = lax.broadcasted_iota(jnp.int32, (OLD, MOVE), 0) == mine
    chosen = jnp.transpose(jnp.where(wanted, jnp.where(low < 3, 1.0, 0.0), 0.0)).astype(BF16)
    for m in range(3):
        for b in range(4):
            columns = slice(b * Q, (b + 1) * Q)
            arr[m, :, columns] = dot(chosen, wts[m, 3 * OLD : 4 * OLD, columns]).astype(BF16)
    arr_copy = pltpu.make_async_copy(arr, arrived, arr_sem)
    arr_copy.start()

    @pl.loop(1, EXPERTS)
    def _(o):
        dispatch(o).wait_send()

    for m in range(3):
        own_side(m, low).wait_send()

    @pl.loop(0, LONG)
    def _(q):
        for d in range(2):
            @pl.when(reaches(d, q))
            def _():
                side(d, q, far).wait_send()

            @pl.when(reaches(d, q) & forwards(d, q))
            def _():
                hop(d, q).wait_send()

            @pl.when(position[d] == 0)
            def _():
                cross(d, q).wait_send()

    acc[...] = jnp.zeros_like(acc)

    @pl.loop(0, EXPERTS // BATCH)
    def _(i):
        @pl.loop(0, BATCH)
        def _(j):
            o = i * BATCH + j

            @pl.when(o > 0)
            def _():
                give_back(o).wait_recv()
                give_back(o).wait_send()

        rows = pl.ds(pl.multiple_of(i * n_rows, n_rows), n_rows)
        end = acc[:, WIDE:]
        for b in range(3):
            columns = slice(b * Q, (b + 1) * Q)
            sums = dot(lhs[b, :, rows], ret[rows, columns])
            acc[:, columns] = acc[:, columns] + (sums[0:128] + sums[128:256])
            end = end + (sums[256:384] + sums[384:512])
        acc[:, WIDE:] = end

    mixed[...] = acc[...].astype(BF16)

    arr_copy.wait()


def on_device(tokens, expert_ids, combine, old_gate, old_up, old_down, move_plan):
    vmem = pl.BlockSpec(memory_space=pltpu.VMEM)
    hbm = pl.BlockSpec(memory_space=pltpu.HBM)
    dma = pltpu.SemaphoreType.DMA
    total = EXPERTS * ROWS

    def stay(array):
        return pltpu.with_memory_space_constraint(array, pltpu.HBM)

    return pl.pallas_call(
        kernel,
        out_shape=(
            jax.ShapeDtypeStruct((TOK, D), BF16),
            jax.ShapeDtypeStruct((3, MOVE, D), BF16),
        ),
        in_specs=[hbm] * 7,
        out_specs=(vmem, hbm),
        scratch_shapes=[
            pltpu.VMEM((8, TOK), jnp.int32),
            pltpu.VMEM((8, TOK), F32),
            pltpu.VMEM((3, EXPERTS, MOVE), jnp.int32),
            pltpu.VMEM((TOK, D), BF16),
            pltpu.VMEM((3, UNITS, D), BF16),
            pltpu.VMEM((total, WIDE), BF16),
            pltpu.VMEM((total, WIDE), BF16),
            pltpu.VMEM((total, WIDE), BF16),
            pltpu.VMEM((total, WIDE), BF16),
            pltpu.VMEM((BATCH * ROWS, UNITS), BF16),
            pltpu.VMEM((BATCH * ROWS, Q), BF16),
            pltpu.VMEM((3, 512, total), BF16),
            pltpu.VMEM((6, BATCH * ROWS, BATCH * ROWS), BF16),
            pltpu.VMEM((3, MOVE, D), BF16),
            pltpu.VMEM((TOK, D), F32),
            dma((4,)),
            dma((3,)),
            dma((EXPERTS,)),
            dma((EXPERTS,)),
            dma((EXPERTS,)),
            dma((EXPERTS,)),
            dma((2, LONG)),
            dma((2, LONG)),
            dma((2, LONG)),
            dma((2, LONG)),
            dma((2, LONG)),
            dma((3,)),
            dma((3,)),
            dma,
        ],
        compiler_params=pltpu.CompilerParams(
            collective_id=0, has_side_effects=True, vmem_limit_bytes=30 * 1024 * 1024
        ),
        name="moe",
    )(
        stay(tokens), stay(expert_ids.T), stay(combine.T), stay(old_gate), stay(old_up), stay(old_down),
        stay(jnp.transpose(move_plan, (1, 0, 2))),
    )


def solution(mesh):
    placed = (
        P(("replica", "expert"), None),
        P(("replica", "expert"), None),
        P(("replica", "expert"), None),
        P("expert", None),
        P("expert", None),
        P("expert", None),
        P(),
    )
    return jax.shard_map(
        on_device,
        mesh=mesh,
        in_specs=placed,
        out_specs=(P(("replica", "expert"), None), P("replica", "expert", None)),
        check_vma=False,
    )
```

```python
import jax
import jax.numpy as jnp
from jax import lax
from jax.experimental import pallas as pl
from jax.experimental.pallas import tpu as pltpu
from jax.sharding import PartitionSpec as P

MESH = pl.DeviceIdType.MESH
F32 = jnp.float32
BF16 = jnp.bfloat16

X, Z, RING, HALF = 4, 8, 8, 4
EXPERTS = X * Z
TOK = 128
D = 2048
Q = D // 4
WIDE = 3 * Q
CAP = 12
ROWS = 16
OLD = 192
UNITS = 4 * OLD
MOVE = 96
PIECES = 18
PIECE = 16
PER = OLD // 2 // PIECE
TAIL = 3
FULL = PIECES - TAIL
LONG = PIECES + TAIL
EARLY = 2 * PER
SKEW = 3
BATCH = 8
NT = (((1,), (1,)), ((), ()))


def dot(a, b):
    return jnp.dot(a, b, preferred_element_type=F32)


def dot_nt(a, b):
    return lax.dot_general(a, b, NT, preferred_element_type=F32)


def one_hot(condition):
    return jnp.where(condition, 1.0, 0.0).astype(BF16)


def z_offset(k):
    odd = lax.rem(k, 2)
    return odd * (HALF + lax.div(k, 2)) + (1 - odd) * lax.rem(HALF - lax.div(k, 2), HALF)


def kernel(
    tokens, expert_ids, combine, gate, up, down, move_plan, mixed, arrived,
    ids, comb, plan, tok, wts, send, recv, outs, ret, hid, x3, lhs, fold, arr, acc,
    in_sem, own_sem, d_send, d_recv, r_send, r_recv, cross_send, hop_send, hop_recv,
    side_send, side_recv, arr_sem,
):
    e = lax.axis_index("expert")
    rep = lax.axis_index("replica")
    low, grp = lax.rem(e, 4), lax.div(e, 4)
    half, core = lax.div(low, 2), lax.rem(low, 2)
    gx, gz = lax.div(grp, Z), lax.rem(grp, Z)
    y = half * HALF + rep
    step = 2 * half - 1
    twin = (e + 1 - 2 * core, rep)

    def peer(o, sign):
        ox, oz = lax.div(o, Z), z_offset(lax.rem(o, Z))
        g = lax.rem(gx + X + sign * ox, X) * Z + lax.rem(gz + Z + sign * oz, Z)
        return (4 * g + low, rep)

    def ring(distance):
        there = lax.rem(y + RING + distance, RING)
        return (4 * grp + 2 * lax.div(there, HALF) + core, lax.rem(there, HALF))

    mats = (gate, up, down)
    fetched = [
        pltpu.make_async_copy(source, target, in_sem.at[i])
        for i, (source, target) in enumerate(((expert_ids, ids), (tokens, tok), (combine, comb), (move_plan, plan)))
    ]
    own = [
        pltpu.make_async_copy(mats[m], wts.at[m, pl.ds(pl.multiple_of(low * OLD, 16), OLD)], own_sem.at[m])
        for m in range(3)
    ]
    for copy in fetched + own:
        copy.start()

    barrier = pltpu.get_barrier_semaphore()

    def greet(device):
        pl.semaphore_signal(barrier, inc=1, device_id=device, device_id_type=MESH)

    @pl.loop(1, EXPERTS)
    def _(o):
        greet(peer(o, 1))

    greet(twin)
    greet(ring(1))
    greet(ring(-1))

    fetched[0].wait()
    ids_t = ids[...]
    row = lax.broadcasted_iota(jnp.int32, (128, 128), 0)
    lane = lax.broadcasted_iota(jnp.int32, (128, 128), 1)
    before = one_hot(row < lane)
    slot = row & 15

    def named(i):
        k = row >> 4
        oz = jnp.where((k & 1) == 1, HALF + (k >> 1), (HALF - (k >> 1)) & 3)
        g = ((gx + i) & 3) * Z + ((gz + oz) & 7)
        return [ids_t[k : k + 1, :] == g for k in range(8)]

    def places(hits):
        member = hits[0]
        for hit in hits[1:]:
            member = member | hit
        rank = dot(one_hot(member), before)
        rank = jnp.where(member, rank, -1.0).astype(jnp.int32)
        first = (rank == slot) & (slot < CAP)
        last = [(rank == 3 * (slot - CAP) + b) & (slot >= CAP) for b in range(3)]
        return first, last

    fetched[1].wait()

    def fill(i):
        first, last = places(named(i))
        rows = pl.ds(pl.multiple_of(i * 128, 128), 128)
        first = one_hot(first)
        for b in range(3):
            part = dot(first, tok[:, b * Q : (b + 1) * Q]) + dot(one_hot(last[b]), tok[:, WIDE:])
            send[rows, b * Q : (b + 1) * Q] = part.astype(BF16)

    fill(0)

    n_rows = BATCH * ROWS
    low_row = lax.broadcasted_iota(jnp.int32, (n_rows, n_rows), 0)
    high_row = lax.broadcasted_iota(jnp.int32, (n_rows, n_rows), 1)
    same = (low_row >> 4) == (high_row >> 4)
    for b in range(3):
        fold[b] = one_hot(
            same & ((low_row & 15) >= CAP) & ((high_row & 15) == 3 * ((low_row & 15) - CAP) + b)
        )
        fold[3 + b] = one_hot(
            same & ((high_row & 15) >= CAP) & ((low_row & 15) == 3 * ((high_row & 15) - CAP) + b)
        )

    pl.semaphore_wait(barrier, EXPERTS + 2)

    def batch_rows(i):
        return pl.ds(pl.multiple_of(i * n_rows, n_rows), n_rows)

    def piece(owner, d, q):
        tail = q >= FULL
        extra = lax.max(q - FULL, 0)
        part = jnp.where(tail, lax.rem(extra, 2), d)
        k = jnp.where(tail, FULL + lax.div(extra, 2), q)
        start = owner * OLD + part * (OLD // 2) + lax.rem(k, PER) * PIECE
        return wts.at[lax.div(k, PER), pl.ds(pl.multiple_of(start, PIECE), PIECE)]

    def passing(ref, sender, receiver, device):
        return pltpu.make_async_remote_copy(
            src_ref=ref, dst_ref=ref, send_sem=sender, recv_sem=receiver, device_id=device, device_id_type=MESH
        )

    position = (half * rep + (1 - half) * (HALF - 1 - rep), half * (HALF - 1 - rep) + (1 - half) * rep)
    ahead = (ring(step), ring(-step))
    behind = (ring(-step), ring(step))
    far = lax.rem(low + 2, 4)

    def cross(d, q):
        return passing(piece(low, d, q), cross_send.at[d], hop_recv.at[d, q], behind[d])

    def hop(d, q):
        return passing(piece(far, d, q), hop_send.at[d], hop_recv.at[d, q], ahead[d])

    def side(d, q, owner):
        return passing(piece(owner, d, q), side_send, side_recv.at[lax.div(q, EARLY)], twin)

    def reaches(d, q):
        return (q >= 0) & (q < LONG) & ((q < FULL) | (position[d] < 2))

    def forwards(d, q):
        return (position[d] == 0) | ((position[d] < HALF - 1) & (q < FULL))

    def own_side(m, owner):
        ref = wts.at[m, pl.ds(pl.multiple_of(owner * OLD, 16), OLD)]
        return passing(ref, side_send, side_recv.at[m // 2], twin)

    for copy in own:
        copy.wait()

    for d in range(2):
        @pl.when(position[d] == 0)
        def _():
            @pl.loop(0, LONG)
            def _(q):
                cross(d, q).start()

    def parcel(source, target, o, sender, receiver, device):
        rows = pl.ds(pl.multiple_of(o * ROWS, ROWS), ROWS)
        return pltpu.make_async_remote_copy(
            src_ref=source.at[rows], dst_ref=target.at[rows], send_sem=sender, recv_sem=receiver.at[lax.div(o, BATCH)],
            device_id=device, device_id_type=MESH,
        )

    def dispatch(o):
        return parcel(send, recv, o, d_send, d_recv, peer(o, 1))

    def give_back(o):
        return parcel(outs, ret, o, r_send, r_recv, peer(o, -1))

    def kept(source, target, receiver):
        return pltpu.make_async_copy(source.at[0:ROWS], target.at[0:ROWS], receiver.at[0])

    def landed(ref, receiver, i):
        rows = batch_rows(i)
        passing(ref.at[rows], d_send, receiver.at[i], twin).wait_recv()

    def left(ref, sender):
        passing(ref, sender, d_recv.at[0], twin).wait_send()

    kept(send, recv, d_recv).start()

    @pl.loop(1, BATCH)
    def _(o):
        dispatch(o).start()

    for m in range(3):
        own_side(m, low).start()

    @pl.loop(1, EXPERTS // BATCH)
    def _(i):
        fill(i)

    @pl.loop(0, FULL + SKEW * (HALF - 1))
    def _(j):
        for d in range(2):
            q = j - SKEW * position[d]

            @pl.when(reaches(d, q))
            def _():
                hop(d, q).wait_recv()

                @pl.when(forwards(d, q))
                def _():
                    hop(d, q).start()

                side(d, q, far).start()

        @pl.when(j < (EXPERTS - BATCH) // 4)
        def _():
            for o in range(4):
                dispatch(BATCH + 4 * j + o).start()

    def side_landed(i):
        rows = wts.at[0] if i == 0 else wts.at[0, 0 : UNITS // 2]
        passing(rows, side_send, side_recv.at[i], twin).wait_recv()

    side_landed(0)
    tiles = UNITS // 256
    out_slot = lax.broadcasted_iota(jnp.int32, (n_rows, Q), 0) & 15

    @pl.loop(0, EXPERTS // BATCH)
    def _(i):
        landed(recv, d_recv, i)
        rows = batch_rows(i)
        tail = dot(fold[3], recv[rows, 0:Q])
        for b in range(1, 3):
            tail = tail + dot(fold[3 + b], recv[rows, b * Q : (b + 1) * Q])
        x3[...] = tail.astype(BF16)

        @pl.loop(0, tiles)
        def _(n):
            units = pl.ds(pl.multiple_of(n * 256, 256), 256)

            def project(m):
                return dot_nt(recv[rows, :], wts[m, units, 0:WIDE]) + dot_nt(x3[...], wts[m, units, WIDE:])

            gate_value = project(0)
            hidden = gate_value / (1.0 + jnp.exp(-gate_value)) * project(1)
            hid[:, units] = hidden.astype(BF16)

        @pl.when(i == 0)
        def _():
            side_landed(1)

        last = dot(hid[...], wts[2, :, WIDE:]).astype(BF16)
        for b in range(3):
            columns = slice(b * Q, (b + 1) * Q)
            value = dot(hid[...], wts[2, :, columns])
            outs[rows, columns] = jnp.where(out_slot < CAP, value, dot(fold[b], last)).astype(BF16)

        @pl.loop(0, BATCH)
        def _(j):
            o = i * BATCH + j

            @pl.when(o > 0)
            def _():
                give_back(o).start()

    kept(outs, ret, r_recv).start()

    fetched[2].wait()
    comb_t = comb[...]

    @pl.loop(0, 4)
    def _(i):
        hits = named(i)
        first, last = places(hits)
        weight = jnp.zeros((128, 128), F32)
        for k in range(8):
            weight = weight + jnp.where(hits[k], comb_t[k : k + 1, :], 0.0)
        columns = pl.ds(pl.multiple_of(i * 128, 128), 128)

        def store(b, at, chosen):
            value = jnp.transpose(jnp.where(chosen, weight, 0.0))
            high = value.astype(BF16)
            lhs[b, at : at + 128, columns] = high
            lhs[b, at + 128 : at + 256, columns] = (value - high.astype(F32)).astype(BF16)

        for b in range(3):
            store(b, 0, first)
            store(b, 256, last[b])

    fetched[3].wait()
    mine = plan[lax.rem(low, 3), pl.ds(grp, 1), :]
    wanted = lax.broadcasted_iota(jnp.int32, (OLD, MOVE), 0) == mine
    chosen = jnp.transpose(jnp.where(wanted, jnp.where(low < 3, 1.0, 0.0), 0.0)).astype(BF16)
    for m in range(3):
        for b in range(4):
            columns = slice(b * Q, (b + 1) * Q)
            arr[m, :, columns] = dot(chosen, wts[m, 3 * OLD : 4 * OLD, columns]).astype(BF16)
    arr_copy = pltpu.make_async_copy(arr, arrived, arr_sem)
    arr_copy.start()

    left(send.at[0 : (EXPERTS - 1) * ROWS], d_send)
    left(wts.at[0:2, 0 : 3 * OLD], side_send)
    for d in range(2):
        @pl.when(position[d] == 0)
        def _():
            left(wts.at[0, 0 : LONG * PIECE], cross_send.at[d])
            left(wts.at[0, 0 : LONG * PIECE], hop_send.at[d])

        @pl.when((position[d] == 1) | (position[d] == 2))
        def _():
            left(wts.at[0, 0 : FULL * PIECE], hop_send.at[d])

    def sums(i, b):
        found = dot(lhs[b, :, batch_rows(i)], ret[batch_rows(i), b * Q : (b + 1) * Q])
        return found[0:128] + found[128:256], found[256:384] + found[384:512]

    acc[...] = jnp.zeros_like(acc)

    @pl.loop(0, EXPERTS // BATCH - 1)
    def _(i):
        landed(ret, r_recv, i)
        end = acc[:, WIDE:]
        for b in range(3):
            columns = slice(b * Q, (b + 1) * Q)
            wide, more = sums(i, b)
            acc[:, columns] = acc[:, columns] + wide
            end = end + more
        acc[:, WIDE:] = end

    final = EXPERTS // BATCH - 1
    landed(ret, r_recv, final)
    end = acc[:, WIDE:]
    for b in range(3):
        columns = slice(b * Q, (b + 1) * Q)
        wide, more = sums(final, b)
        mixed[:, columns] = (acc[:, columns] + wide).astype(BF16)
        end = end + more
    mixed[:, WIDE:] = end.astype(BF16)
    left(outs.at[0 : (EXPERTS - 1) * ROWS], r_send)
    arr_copy.wait()


def on_device(tokens, expert_ids, combine, old_gate, old_up, old_down, move_plan):
    vmem = pl.BlockSpec(memory_space=pltpu.VMEM)
    hbm = pl.BlockSpec(memory_space=pltpu.HBM)
    dma = pltpu.SemaphoreType.DMA
    total = EXPERTS * ROWS

    def stay(array):
        return pltpu.with_memory_space_constraint(array, pltpu.HBM)

    return pl.pallas_call(
        kernel,
        out_shape=(
            jax.ShapeDtypeStruct((TOK, D), BF16),
            jax.ShapeDtypeStruct((3, MOVE, D), BF16),
        ),
        in_specs=[hbm] * 7,
        out_specs=(vmem, hbm),
        scratch_shapes=[
            pltpu.VMEM((8, TOK), jnp.int32),
            pltpu.VMEM((8, TOK), F32),
            pltpu.VMEM((3, EXPERTS, MOVE), jnp.int32),
            pltpu.VMEM((TOK, D), BF16),
            pltpu.VMEM((3, UNITS, D), BF16),
            pltpu.VMEM((total, WIDE), BF16),
            pltpu.VMEM((total, WIDE), BF16),
            pltpu.VMEM((total, WIDE), BF16),
            pltpu.VMEM((total, WIDE), BF16),
            pltpu.VMEM((BATCH * ROWS, UNITS), BF16),
            pltpu.VMEM((BATCH * ROWS, Q), BF16),
            pltpu.VMEM((3, 512, total), BF16),
            pltpu.VMEM((6, BATCH * ROWS, BATCH * ROWS), BF16),
            pltpu.VMEM((3, MOVE, D), BF16),
            pltpu.VMEM((TOK, D), F32),
            dma((4,)),
            dma((3,)),
            dma,
            dma((EXPERTS // BATCH,)),
            dma,
            dma((EXPERTS // BATCH,)),
            dma((2,)),
            dma((2,)),
            dma((2, LONG)),
            dma,
            dma((2,)),
            dma,
        ],
        compiler_params=pltpu.CompilerParams(
            collective_id=0, has_side_effects=True, vmem_limit_bytes=30 * 1024 * 1024
        ),
        name="moe",
    )(
        stay(tokens), stay(expert_ids.T), stay(combine.T), stay(old_gate), stay(old_up), stay(old_down),
        stay(jnp.transpose(move_plan, (1, 0, 2))),
    )


def solution(mesh):
    placed = (
        P(("replica", "expert"), None),
        P(("replica", "expert"), None),
        P(("replica", "expert"), None),
        P("expert", None),
        P("expert", None),
        P("expert", None),
        P(),
    )
    return jax.shard_map(
        on_device,
        mesh=mesh,
        in_specs=placed,
        out_specs=(P(("replica", "expert"), None), P("replica", "expert", None)),
        check_vma=False,
    )
```

```python
import jax
import jax.numpy as jnp
from jax import lax
from jax.experimental import pallas as pl
from jax.experimental.pallas import tpu as pltpu
from jax.sharding import PartitionSpec as P

MESH = pl.DeviceIdType.MESH
F32 = jnp.float32
BF16 = jnp.bfloat16

X, Z, RING, HALF = 4, 8, 8, 4
EXPERTS = X * Z
TOK = 128
D = 2048
Q = D // 4
WIDE = 3 * Q
CAP = 12
ROWS = 16
OLD = 192
UNITS = 4 * OLD
MOVE = 96
PIECES = 18
PIECE = 16
PER = OLD // 2 // PIECE
TAIL = 3
FULL = PIECES - TAIL
LONG = PIECES + TAIL
EARLY = 2 * PER
SKEW = 3
PACE = 5
BATCH = 8
NT = (((1,), (1,)), ((), ()))


def dot(a, b):
    return jnp.dot(a, b, preferred_element_type=F32)


def dot_nt(a, b):
    return lax.dot_general(a, b, NT, preferred_element_type=F32)


def one_hot(condition):
    return jnp.where(condition, 1.0, 0.0).astype(BF16)


def z_offset(k):
    odd = lax.rem(k, 2)
    return odd * (HALF + lax.div(k, 2)) + (1 - odd) * lax.rem(HALF - lax.div(k, 2), HALF)


def kernel(
    tokens, expert_ids, combine, gate, up, down, move_plan, mixed, arrived,
    ids, comb, plan, tok, wts, send, recv, outs, ret, hid, x3, lhs, fold, arr, acc,
    in_sem, own_sem, d_send, d_recv, r_send, r_recv, cross_send, hop_send, hop_recv,
    side_send, side_recv, arr_sem,
):
    e = lax.axis_index("expert")
    rep = lax.axis_index("replica")
    low, grp = lax.rem(e, 4), lax.div(e, 4)
    half, core = lax.div(low, 2), lax.rem(low, 2)
    gx, gz = lax.div(grp, Z), lax.rem(grp, Z)
    y = half * HALF + rep
    step = 2 * half - 1
    twin = (e + 1 - 2 * core, rep)

    def peer(o, sign):
        ox, oz = lax.div(o, Z), z_offset(lax.rem(o, Z))
        g = lax.rem(gx + X + sign * ox, X) * Z + lax.rem(gz + Z + sign * oz, Z)
        return (4 * g + low, rep)

    def ring(distance):
        there = lax.rem(y + RING + distance, RING)
        return (4 * grp + 2 * lax.div(there, HALF) + core, lax.rem(there, HALF))

    mats = (gate, up, down)
    fetched = [
        pltpu.make_async_copy(source, target, in_sem.at[i])
        for i, (source, target) in enumerate(((expert_ids, ids), (tokens, tok), (combine, comb), (move_plan, plan)))
    ]
    own = [
        pltpu.make_async_copy(mats[m], wts.at[m, pl.ds(pl.multiple_of(low * OLD, 16), OLD)], own_sem.at[m])
        for m in range(3)
    ]
    for copy in own + fetched:
        copy.start()

    barrier = pltpu.get_barrier_semaphore()

    def greet(device):
        pl.semaphore_signal(barrier, inc=1, device_id=device, device_id_type=MESH)

    @pl.loop(1, EXPERTS)
    def _(o):
        greet(peer(o, 1))

    greet(twin)
    greet(ring(1))
    greet(ring(-1))

    pl.semaphore_wait(barrier, EXPERTS + 2)

    n_rows = BATCH * ROWS

    def batch_rows(i):
        return pl.ds(pl.multiple_of(i * n_rows, n_rows), n_rows)

    def piece(owner, d, q):
        tail = q >= FULL
        extra = lax.max(q - FULL, 0)
        part = jnp.where(tail, lax.rem(extra, 2), d)
        k = jnp.where(tail, FULL + lax.div(extra, 2), q)
        start = owner * OLD + part * (OLD // 2) + lax.rem(k, PER) * PIECE
        return wts.at[lax.div(k, PER), pl.ds(pl.multiple_of(start, PIECE), PIECE)]

    def passing(ref, sender, receiver, device):
        return pltpu.make_async_remote_copy(
            src_ref=ref, dst_ref=ref, send_sem=sender, recv_sem=receiver, device_id=device, device_id_type=MESH
        )

    place = half * rep + (1 - half) * (HALF - 1 - rep)
    early = lax.div(place, 2)
    position = ((1 - early) * place + early * (HALF - 1 - place), early * place + (1 - early) * (HALF - 1 - place))
    way = step * (1 - 2 * early)
    direction = (early, 1 - early)
    ahead = (ring(way), ring(-way))
    behind = (ring(-way), ring(way))
    far = lax.rem(low + 2, 4)

    def cross(d, q):
        return passing(piece(low, direction[d], q), cross_send, hop_recv.at[direction[d], q], behind[d])

    def hop(d, q):
        return passing(piece(far, direction[d], q), hop_send.at[d], hop_recv.at[direction[d], q], ahead[d])

    def side(d, q, owner):
        return passing(piece(owner, direction[d], q), side_send, side_recv.at[lax.div(q, EARLY)], twin)

    def reaches(d, q):
        return (q >= 0) & (q < (LONG if d == 0 else FULL))

    def forwards(d, q):
        return ((position[0] == 0) | (q < FULL)) if d == 0 else (position[1] == 2)

    def own_side(m, owner):
        ref = wts.at[m, pl.ds(pl.multiple_of(owner * OLD, 16), OLD)]
        return passing(ref, side_send, side_recv.at[m // 2], twin)

    for copy in own:
        copy.wait()

    def cross_from(first, last):
        @pl.when(position[0] == 0)
        def _():
            @pl.loop(first, last)
            def _(q):
                cross(0, q).start()

    cross_from(0, 4)

    fetched[0].wait()
    ids_t = ids[...]
    row = lax.broadcasted_iota(jnp.int32, (128, 128), 0)
    lane = lax.broadcasted_iota(jnp.int32, (128, 128), 1)
    before = one_hot(row < lane)
    slot = row & 15

    def named(i):
        k = row >> 4
        oz = jnp.where((k & 1) == 1, HALF + (k >> 1), (HALF - (k >> 1)) & 3)
        g = ((gx + i) & 3) * Z + ((gz + oz) & 7)
        return [ids_t[k : k + 1, :] == g for k in range(8)]

    def places(hits):
        member = hits[0]
        for hit in hits[1:]:
            member = member | hit
        rank = dot(one_hot(member), before)
        rank = jnp.where(member, rank, -1.0).astype(jnp.int32)
        first = (rank == slot) & (slot < CAP)
        last = [(rank == 3 * (slot - CAP) + b) & (slot >= CAP) for b in range(3)]
        return first, last

    fetched[1].wait()

    def fill(i):
        first, last = places(named(i))
        rows = pl.ds(pl.multiple_of(i * 128, 128), 128)
        first = one_hot(first)
        for b in range(3):
            part = dot(first, tok[:, b * Q : (b + 1) * Q]) + dot(one_hot(last[b]), tok[:, WIDE:])
            send[rows, b * Q : (b + 1) * Q] = part.astype(BF16)

    fill(0)

    def parcel(source, target, o, sender, receiver, device):
        rows = pl.ds(pl.multiple_of(o * ROWS, ROWS), ROWS)
        return pltpu.make_async_remote_copy(
            src_ref=source.at[rows], dst_ref=target.at[rows], send_sem=sender, recv_sem=receiver.at[lax.div(o, BATCH)],
            device_id=device, device_id_type=MESH,
        )

    def dispatch(o):
        return parcel(send, recv, o, d_send, d_recv, peer(o, 1))

    def give_back(o):
        return parcel(outs, ret, o, r_send, r_recv, peer(o, -1))

    def kept(source, target, receiver):
        return pltpu.make_async_copy(source.at[0:ROWS], target.at[0:ROWS], receiver.at[0])

    def landed(ref, receiver, i):
        rows = batch_rows(i)
        passing(ref.at[rows], d_send, receiver.at[i], twin).wait_recv()

    def left(ref, sender):
        passing(ref, sender, d_recv.at[0], twin).wait_send()

    kept(send, recv, d_recv).start()

    @pl.loop(1, BATCH)
    def _(o):
        dispatch(o).start()

    cross_from(4, LONG)
    for m in range(3):
        own_side(m, low).start()

    low_row = lax.broadcasted_iota(jnp.int32, (n_rows, n_rows), 0)
    high_row = lax.broadcasted_iota(jnp.int32, (n_rows, n_rows), 1)
    same = (low_row >> 4) == (high_row >> 4)
    for b in range(3):
        fold[b] = one_hot(
            same & ((low_row & 15) >= CAP) & ((high_row & 15) == 3 * ((low_row & 15) - CAP) + b)
        )
        fold[3 + b] = one_hot(
            same & ((high_row & 15) >= CAP) & ((low_row & 15) == 3 * ((high_row & 15) - CAP) + b)
        )

    @pl.loop(0, max(FULL + SKEW * (HALF - 1), LONG + SKEW))
    def _(j):
        for d in range(2):
            q = j - SKEW * position[d]

            @pl.when(reaches(d, q))
            def _():
                hop(d, q).wait_recv()

                @pl.when(forwards(d, q))
                def _():
                    hop(d, q).start()

                side(d, q, far).start()

        @pl.when((j < PACE * (EXPERTS // BATCH - 1)) & (lax.rem(j, PACE) == 0))
        def _():
            i = lax.div(j, PACE) + 1
            fill(i)

            @pl.loop(0, BATCH)
            def _(o):
                dispatch(i * BATCH + o).start()

    def side_landed(i):
        rows = wts.at[0] if i == 0 else wts.at[0, 0 : UNITS // 2]
        passing(rows, side_send, side_recv.at[i], twin).wait_recv()

    side_landed(0)
    tiles = UNITS // 256
    out_slot = lax.broadcasted_iota(jnp.int32, (n_rows, Q), 0) & 15

    @pl.loop(0, EXPERTS // BATCH)
    def _(i):
        landed(recv, d_recv, i)
        rows = batch_rows(i)
        tail = dot(fold[3], recv[rows, 0:Q])
        for b in range(1, 3):
            tail = tail + dot(fold[3 + b], recv[rows, b * Q : (b + 1) * Q])
        x3[...] = tail.astype(BF16)

        @pl.loop(0, tiles)
        def _(n):
            units = pl.ds(pl.multiple_of(n * 256, 256), 256)

            def project(m):
                return dot_nt(recv[rows, :], wts[m, units, 0:WIDE]) + dot_nt(x3[...], wts[m, units, WIDE:])

            gate_value = project(0)
            hidden = gate_value / (1.0 + jnp.exp(-gate_value)) * project(1)
            hid[:, units] = hidden.astype(BF16)

        @pl.when(i == 0)
        def _():
            side_landed(1)

        last = dot(hid[...], wts[2, :, WIDE:]).astype(BF16)
        for b in range(3):
            columns = slice(b * Q, (b + 1) * Q)
            value = dot(hid[...], wts[2, :, columns])
            outs[rows, columns] = jnp.where(out_slot < CAP, value, dot(fold[b], last)).astype(BF16)

        @pl.loop(0, BATCH)
        def _(j):
            o = i * BATCH + j

            @pl.when(o > 0)
            def _():
                give_back(o).start()

    kept(outs, ret, r_recv).start()

    fetched[2].wait()
    comb_t = comb[...]

    @pl.loop(0, 4)
    def _(i):
        hits = named(i)
        first, last = places(hits)
        weight = jnp.zeros((128, 128), F32)
        for k in range(8):
            weight = weight + jnp.where(hits[k], comb_t[k : k + 1, :], 0.0)
        columns = pl.ds(pl.multiple_of(i * 128, 128), 128)

        def store(b, at, chosen):
            value = jnp.transpose(jnp.where(chosen, weight, 0.0))
            high = value.astype(BF16)
            lhs[b, at : at + 128, columns] = high
            lhs[b, at + 128 : at + 256, columns] = (value - high.astype(F32)).astype(BF16)

        for b in range(3):
            store(b, 0, first)
            store(b, 256, last[b])

    fetched[3].wait()
    mine = plan[lax.rem(low, 3), pl.ds(grp, 1), :]
    wanted = lax.broadcasted_iota(jnp.int32, (OLD, MOVE), 0) == mine
    chosen = jnp.transpose(jnp.where(wanted, jnp.where(low < 3, 1.0, 0.0), 0.0)).astype(BF16)
    for m in range(3):
        for b in range(4):
            columns = slice(b * Q, (b + 1) * Q)
            arr[m, :, columns] = dot(chosen, wts[m, 3 * OLD : 4 * OLD, columns]).astype(BF16)
    arr_copy = pltpu.make_async_copy(arr, arrived, arr_sem)
    arr_copy.start()

    left(send.at[0 : (EXPERTS - 1) * ROWS], d_send)
    left(wts.at[0:2, 0 : 3 * OLD], side_send)
    @pl.when(position[0] == 0)
    def _():
        left(wts.at[0, 0 : LONG * PIECE], cross_send)
        left(wts.at[0, 0 : LONG * PIECE], hop_send.at[0])

    @pl.when(position[0] == 1)
    def _():
        left(wts.at[0, 0 : FULL * PIECE], hop_send.at[0])
        left(wts.at[0, 0 : FULL * PIECE], hop_send.at[1])

    def sums(i, b):
        found = dot(lhs[b, :, batch_rows(i)], ret[batch_rows(i), b * Q : (b + 1) * Q])
        return found[0:128] + found[128:256], found[256:384] + found[384:512]

    acc[...] = jnp.zeros_like(acc)

    @pl.loop(0, EXPERTS // BATCH - 1)
    def _(i):
        landed(ret, r_recv, i)
        end = acc[:, WIDE:]
        for b in range(3):
            columns = slice(b * Q, (b + 1) * Q)
            wide, more = sums(i, b)
            acc[:, columns] = acc[:, columns] + wide
            end = end + more
        acc[:, WIDE:] = end

    final = EXPERTS // BATCH - 1
    landed(ret, r_recv, final)
    end = acc[:, WIDE:]
    for b in range(3):
        columns = slice(b * Q, (b + 1) * Q)
        wide, more = sums(final, b)
        mixed[:, columns] = (acc[:, columns] + wide).astype(BF16)
        end = end + more
    mixed[:, WIDE:] = end.astype(BF16)
    left(outs.at[0 : (EXPERTS - 1) * ROWS], r_send)
    arr_copy.wait()


def on_device(tokens, expert_ids, combine, old_gate, old_up, old_down, move_plan):
    vmem = pl.BlockSpec(memory_space=pltpu.VMEM)
    hbm = pl.BlockSpec(memory_space=pltpu.HBM)
    dma = pltpu.SemaphoreType.DMA
    total = EXPERTS * ROWS

    def stay(array):
        return pltpu.with_memory_space_constraint(array, pltpu.HBM)

    return pl.pallas_call(
        kernel,
        out_shape=(
            jax.ShapeDtypeStruct((TOK, D), BF16),
            jax.ShapeDtypeStruct((3, MOVE, D), BF16),
        ),
        in_specs=[hbm] * 7,
        out_specs=(vmem, hbm),
        scratch_shapes=[
            pltpu.VMEM((8, TOK), jnp.int32),
            pltpu.VMEM((8, TOK), F32),
            pltpu.VMEM((3, EXPERTS, MOVE), jnp.int32),
            pltpu.VMEM((TOK, D), BF16),
            pltpu.VMEM((3, UNITS, D), BF16),
            pltpu.VMEM((total, WIDE), BF16),
            pltpu.VMEM((total, WIDE), BF16),
            pltpu.VMEM((total, WIDE), BF16),
            pltpu.VMEM((total, WIDE), BF16),
            pltpu.VMEM((BATCH * ROWS, UNITS), BF16),
            pltpu.VMEM((BATCH * ROWS, Q), BF16),
            pltpu.VMEM((3, 512, total), BF16),
            pltpu.VMEM((6, BATCH * ROWS, BATCH * ROWS), BF16),
            pltpu.VMEM((3, MOVE, D), BF16),
            pltpu.VMEM((TOK, D), F32),
            dma((4,)),
            dma((3,)),
            dma,
            dma((EXPERTS // BATCH,)),
            dma,
            dma((EXPERTS // BATCH,)),
            dma,
            dma((2,)),
            dma((2, LONG)),
            dma,
            dma((2,)),
            dma,
        ],
        compiler_params=pltpu.CompilerParams(
            collective_id=0, has_side_effects=True, vmem_limit_bytes=30 * 1024 * 1024
        ),
        name="moe",
    )(
        stay(tokens), stay(expert_ids.T), stay(combine.T), stay(old_gate), stay(old_up), stay(old_down),
        stay(jnp.transpose(move_plan, (1, 0, 2))),
    )


def solution(mesh):
    placed = (
        P(("replica", "expert"), None),
        P(("replica", "expert"), None),
        P(("replica", "expert"), None),
        P("expert", None),
        P("expert", None),
        P("expert", None),
        P(),
    )
    return jax.shard_map(
        on_device,
        mesh=mesh,
        in_specs=placed,
        out_specs=(P(("replica", "expert"), None), P("replica", "expert", None)),
        check_vma=False,
    )
```
